32 devices in a mesh: node: 16 (over z, y, core), local: 2 (over x).
Axes of the slice: x: 2, y: 2, z: 4, core: 2. Of those that a mesh axis runs over, the one named last changes fastest.
Arguments:
- block_input: bfloat16 [12544, 512], P(('node', 'local')), may hold values from 0 to 2
- conv_weight: bfloat16 [512, 2048], replicated, may hold values from -0.25 to 0.25
- bn_gain: float32 [2048], replicated, may hold values from 0.1 to 1.9
- out_cotangent: bfloat16 [12544, 2048], P(('node', 'local')), may hold values from -0.109375 to 0.109375
- master_weight: float32 [2048, 512], P('node'), may hold values from -0.25 to 0.25
- velocity: float32 [2048, 512], P('node'), may hold values from -6 to 6
Outputs:
- new_velocity: float32 [2048, 512], P('node')
- new_weight: float32 [2048, 512], P('node')
The draws below stay inside these ranges and needn't reach their ends.
All inputs are finite; a program needn't handle non-finite values.
Results may differ from the reference program's by a relative error of at most 0.0095.
Values may be sent and summed in bfloat16 or wider, within the bound.
No kernel may reach another device: no remote copies, remote signals or barrier semaphores. Data moves between devices by JAX's collectives and lax.ppermute only.
A program may use at most 64 MiB of HBM per device.

```python
import jax
import jax.numpy as jnp
from jax import lax

CIN = 512
COUT = 2048
ROWS_DEV = 392
ROWS = 12544
DEVICES = 32


def spiked(values, stream_key, source, target, parts, factor):
    def block_of(dim):
        return (jnp.arange(values.shape[dim]) // (values.shape[dim] // parts)).reshape((-1,) + (1,) * (values.ndim - 1 - dim))

    first = jax.random.permutation(stream_key, parts)[block_of(target)]
    far = (block_of(target) + parts // 2) % parts
    return jnp.where((block_of(source) == first) | (block_of(source) == far), factor * values, values)


def steps_of(own_key, shape, split, least, largest):
    level, own = 1.0, jax.random.fold_in(own_key, 6)
    for position, blocks in split:
        heights = jnp.exp(jax.random.uniform(jax.random.fold_in(own, position), (blocks,), jnp.float32, least / len(split), largest / len(split)))
        level = level * jnp.repeat(heights, shape[position] // blocks).reshape([-1 if axis == position else 1 for axis in range(len(shape))])
    return level


def bell_draw(own_key, shape, scale, limit, split=(), dtype=jnp.bfloat16):
    values = jax.random.normal(own_key, shape, jnp.float32) * scale
    if len(split) > 0:
        values = steps_of(own_key, shape, split, -0.22, 0.18) * values
    return jnp.clip(values, min=-limit, max=limit).astype(dtype)


def noise_with(own_key, shape, width, reach, cuts, heavy, kind=jnp.bfloat16):
    entries = width * jax.random.normal(own_key, shape, jnp.float32)
    if cuts:
        entries = entries * steps_of(own_key, shape, cuts, -0.22, 0.18)
    return jnp.clip(spiked(entries, jax.random.fold_in(own_key, 3), *heavy), -reach, reach).astype(kind)


def setup_inputs(seed: int = 0) -> dict:
    keys = jax.random.split(jax.random.key(seed), 7)
    return {
        "block_input": jnp.clip(2.0 * jax.random.uniform(keys[0], (ROWS, CIN), jnp.float32) ** steps_of(keys[0], (ROWS, CIN), ((0, 32),), -0.2, 0.2), 0.0, 2.0).astype(jnp.bfloat16),
        "conv_weight": bell_draw(keys[1], (CIN, COUT), CIN ** -0.5, 0.25),
        "bn_gain": jnp.clip(1.0 + 0.18 * jax.random.normal(keys[2], (COUT,), jnp.float32), 0.1, 1.9),
        "out_cotangent": noise_with(keys[3], (ROWS, COUT), ((ROWS_DEV * DEVICES) ** -0.5), 0.109375, ((0, 32),), (0, 1, 32, 2.75)),
        "master_weight": bell_draw(keys[4], (COUT, CIN), CIN ** -0.5, 0.25, ((0, 16),), jnp.float32),
        "velocity": bell_draw(keys[5], (COUT, CIN), 1.0, 6.0, ((0, 16),), jnp.float32),
    }


EPS = 1e-05
MOMENTUM = 0.9
RATE = 0.1
DECAY = 5e-05

def reference(block_input, conv_weight, bn_gain, out_cotangent, master_weight, velocity):
    inputs = block_input.reshape(DEVICES, ROWS_DEV, CIN)
    cotangents = out_cotangent.reshape(DEVICES, ROWS_DEV, COUT)

    def device_term(accumulated, pieces):
        activations, cotangent = pieces
        convolved = jnp.dot(activations, conv_weight, preferred_element_type=jnp.float32)
        center = lax.optimization_barrier(jnp.mean(convolved, axis=0))
        spread = convolved - center
        inverse = lax.rsqrt(lax.optimization_barrier(jnp.mean(spread * spread, axis=0)) + EPS)
        normed = spread * inverse
        upstream = cotangent.astype(jnp.float32)
        shift_grad = lax.optimization_barrier(jnp.sum(upstream, axis=0))
        gain_grad = lax.optimization_barrier(jnp.sum(upstream * normed, axis=0))
        conv_grad = (bn_gain * inverse / ROWS_DEV * (ROWS_DEV * upstream - shift_grad - normed * gain_grad)).astype(jnp.bfloat16)
        contribution = lax.dot_general(conv_grad, activations, (((0,), (0,)), ((), ())), preferred_element_type=jnp.float32)
        contribution = lax.optimization_barrier(contribution.astype(jnp.bfloat16)).astype(jnp.float32)
        return (accumulated + contribution, None)
    gradient, _ = lax.scan(device_term, jnp.zeros((COUT, CIN), jnp.float32), (inputs, cotangents))
    new_velocity = MOMENTUM * velocity + gradient + DECAY * master_weight
    new_weight = master_weight - RATE * new_velocity
    return (new_velocity, new_weight)
```

```python
import functools

import jax
import jax.numpy as jnp
from jax import lax
from jax.experimental import pallas as pl
from jax.experimental.pallas import tpu as pltpu
from jax.sharding import PartitionSpec as P

EPS = 1e-05
MOMENTUM = 0.9
RATE = 0.1
DECAY = 5e-05

BLOCK = 256
CHUNKS = 2
NODE = "node"
LOCAL = "local"


def term_kernel(run, core_ref, x_ref, w_ref, gain_ref, u_ref, mine_ref, other_ref, term_ref):
    core = core_ref[0]
    rows = x_ref.shape[0]
    x = x_ref[...]
    conv = jnp.dot(x, w_ref[...], preferred_element_type=jnp.float32)
    center = jnp.sum(conv, axis=0, keepdims=True) * (1.0 / rows)
    spread = conv - center
    upstream = u_ref[...].astype(jnp.float32)
    inverse = lax.rsqrt(jnp.sum(spread * spread, axis=0, keepdims=True) * (1.0 / rows) + EPS)
    shift_grad = jnp.sum(upstream, axis=0, keepdims=True)
    gain_grad = jnp.sum(upstream * spread, axis=0, keepdims=True) * inverse
    scale = gain_ref[...] * inverse
    step = scale * (1.0 / rows)
    grad = scale * upstream - (step * shift_grad + spread * (step * inverse * gain_grad))
    term_ref[...] = lax.dot_general(
        grad.astype(jnp.bfloat16), x, (((0,), (0,)), ((), ())), preferred_element_type=jnp.float32
    )
    for pair in range(term_ref.shape[0] // (2 * run)):
        own = pl.multiple_of(pair * 2 * run + core * run, run)
        far = pl.multiple_of(pair * 2 * run + (1 - core) * run, run)
        mine_ref[pl.ds(pair * run, run), :] = term_ref[pl.ds(own, run), :].astype(jnp.bfloat16)
        other_ref[pl.ds(pair * run, run), :] = term_ref[pl.ds(far, run), :].astype(jnp.bfloat16)


def term_chunk(chunk, run, core, block_input, conv_weight, gain, out_cotangent):
    rows, width_in = block_input.shape
    width_out = conv_weight.shape[1]
    channels = width_out // CHUNKS
    steps = channels // BLOCK
    first = chunk * steps
    out = jax.ShapeDtypeStruct((channels // 2, width_in), jnp.bfloat16)
    return pl.pallas_call(
        functools.partial(term_kernel, run),
        grid=(steps,),
        out_shape=(out, out),
        in_specs=[
            pl.BlockSpec(memory_space=pltpu.SMEM),
            pl.BlockSpec((rows, width_in), lambda i: (0, 0)),
            pl.BlockSpec((width_in, BLOCK), lambda i: (0, first + i)),
            pl.BlockSpec((1, BLOCK), lambda i: (0, first + i)),
            pl.BlockSpec((rows, BLOCK), lambda i: (0, first + i)),
        ],
        out_specs=(
            pl.BlockSpec((BLOCK // 2, width_in), lambda i: (i, 0)),
            pl.BlockSpec((BLOCK // 2, width_in), lambda i: (i, 0)),
        ),
        scratch_shapes=[pltpu.VMEM((BLOCK, width_in), jnp.float32)],
        cost_estimate=pl.CostEstimate(
            flops=4 * rows * channels * width_in,
            bytes_accessed=2 * (rows * channels + channels * width_in * 2 + rows * width_in),
            transcendentals=channels,
        ),
        compiler_params=pltpu.CompilerParams(vmem_limit_bytes=24 * 2**20),
        name="term_chunk",
    )(core, block_input, conv_weight, gain, out_cotangent)


def pick(array, index, axis):
    return lax.dynamic_index_in_dim(array, index, axis, keepdims=False)


def shift_pairs(size, shift):
    return [(i, (i + shift) % size) for i in range(size)]


def flip_pairs(size, bit):
    return [(i, i ^ bit) for i in range(size)]


def local_fn(block_input, conv_weight, bn_gain, out_cotangent, master_weight, velocity):
    f32, bf16 = jnp.float32, jnp.bfloat16
    nodes = lax.axis_size(NODE)
    locals_ = lax.axis_size(LOCAL)
    width_in = block_input.shape[1]
    width_out = conv_weight.shape[1]
    run = width_out // nodes
    part = run // locals_
    node = lax.axis_index(NODE)
    lane = lax.axis_index(LOCAL)
    core = node % 2
    side = (node // 2) % 2
    deep = node // 4
    depth = nodes // 4
    half = depth // CHUNKS

    gain = bn_gain.reshape(1, width_out)
    core_arg = core.astype(jnp.int32).reshape(1)

    def core_swap(array):
        return lax.ppermute(array, NODE, flip_pairs(nodes, 1))

    def side_swap(array):
        return lax.ppermute(array, NODE, flip_pairs(nodes, 2))

    def lane_reduce(send, keep):
        total = keep
        for shift in range(1, locals_):
            arrived = lax.ppermute(
                send((lane + shift) % locals_), LOCAL, shift_pairs(locals_, shift)
            )
            total = total + arrived.astype(f32)
        return total

    shape = (half, 2, locals_, part, width_in)
    mine, got = [], []
    for chunk in range(CHUNKS):
        a, b = term_chunk(chunk, run, core_arg, block_input, conv_weight, gain, out_cotangent)
        mine.append(a.reshape(shape))
        got.append(core_swap(b).reshape(shape))

    def chip(chunk, side_index, lane_index):
        a, b = mine[chunk], got[chunk]
        if lane_index is not None:
            a, b = pick(a, lane_index, 2), pick(b, lane_index, 2)
        if side_index is not None:
            a, b = pick(a, side_index, 1), pick(b, side_index, 1)
        return a.astype(f32) + b.astype(f32)

    over_x = lane_reduce(lambda l: chip(0, None, l).astype(bf16), chip(0, None, lane))
    arrived = side_swap(chip(1, 1 - side, None).astype(bf16))
    over_y = chip(1, side, None) + arrived.astype(f32)

    arrived = side_swap(pick(over_x, 1 - side, 1).astype(bf16))
    first = pick(over_x, side, 1) + arrived.astype(f32)
    second = lane_reduce(lambda l: pick(over_y, l, 1).astype(bf16), pick(over_y, lane, 1))

    plane = jnp.concatenate([first, second], axis=0)
    total = pick(plane, deep, 0)
    for shift in range(1, depth):
        piece = pick(plane, (deep + shift) % depth, 0).astype(bf16)
        arrived = lax.ppermute(piece, NODE, shift_pairs(nodes, 4 * shift))
        total = total + arrived.astype(f32)

    total = total.astype(bf16)
    pieces = [total]
    for shift in range(1, locals_):
        pieces.append(lax.ppermute(total, LOCAL, shift_pairs(locals_, -shift)))
    gradient = jnp.concatenate(
        [
            functools.reduce(
                lambda other, s: jnp.where((lane + s) % locals_ == l, pieces[s], other),
                range(1, locals_),
                pieces[0],
            )
            for l in range(locals_)
        ],
        axis=0,
    ).astype(f32)
    new_velocity = MOMENTUM * velocity + gradient + DECAY * master_weight
    new_weight = master_weight - RATE * new_velocity
    return (new_velocity, new_weight)


def solution(mesh):
    in_specs = (
        P((NODE, LOCAL), None),
        P(),
        P(),
        P((NODE, LOCAL), None),
        P(NODE, None),
        P(NODE, None),
    )
    out_specs = (P(NODE, None), P(NODE, None))
    return jax.shard_map(local_fn, mesh=mesh, in_specs=in_specs, out_specs=out_specs, check_vma=False)
```

```python
import functools

import jax
import jax.numpy as jnp
from jax import lax
from jax.experimental import pallas as pl
from jax.experimental.pallas import tpu as pltpu
from jax.sharding import PartitionSpec as P

EPS = 1e-05
MOMENTUM = 0.9
RATE = 0.1
DECAY = 5e-05

TILE = 128
PACK = 16
NODE = "node"
LOCAL = "local"
F32 = jnp.float32
BF16 = jnp.bfloat16


def term_rows(x, weight, gain, cotangent):
    rows = x.shape[0]
    conv = jnp.dot(x, weight, preferred_element_type=F32)
    center = jnp.sum(conv, axis=0, keepdims=True) * (1.0 / rows)
    spread = conv - center
    upstream = cotangent.astype(F32)
    inverse = lax.rsqrt(jnp.sum(spread * spread, axis=0, keepdims=True) * (1.0 / rows) + EPS)
    shift_grad = jnp.sum(upstream, axis=0, keepdims=True)
    gain_grad = jnp.sum(upstream * spread, axis=0, keepdims=True) * inverse
    scale = gain * inverse
    step = scale * (1.0 / rows)
    grad = scale * upstream - (step * shift_grad + spread * (step * inverse * gain_grad))
    return lax.dot_general(
        grad.astype(BF16), x, (((0,), (0,)), ((), ())), preferred_element_type=F32
    ).astype(BF16)


def store_rows(orders, out_refs, x_ref, w_ref, gain_ref, u_ref):
    blocks = len(out_refs)
    block = w_ref.shape[1] // blocks
    for b in range(blocks):
        columns = slice(b * block, (b + 1) * block)
        term = term_rows(x_ref[...], w_ref[:, columns], gain_ref[:, columns], u_ref[:, columns])
        for source, target, count in orders[b]:
            out_refs[b][target : target + count] = term[source : source + count]


def term_kernel(
    piece, orders, sel_ref, x_hbm, w_hbm, gain_hbm, u_hbm, a_ref, b_ref, x_ref, w_ref, gain_ref, u_ref, sem
):
    parity = sel_ref[0]
    copies = [pltpu.make_async_copy(x_hbm, x_ref, sem.at[0])]
    for j in range(w_ref.shape[1] // piece):
        source = pl.ds(pl.multiple_of((2 * j + parity) * piece, piece), piece)
        target = pl.ds(j * piece, piece)
        for a, b in ((w_hbm, w_ref), (u_hbm, u_ref), (gain_hbm, gain_ref)):
            copies.append(pltpu.make_async_copy(a.at[:, source], b.at[:, target], sem.at[len(copies)]))
    for copy in copies:
        copy.start()
    for copy in copies:
        copy.wait()
    store_rows(orders, (a_ref, b_ref), x_ref, w_ref, gain_ref, u_ref)


def terms(piece, orders, parity, block_input, conv_weight, gain, out_cotangent, name):
    rows, width_in = block_input.shape
    channels = conv_weight.shape[1] // 2
    hbm = pl.BlockSpec(memory_space=pltpu.HBM)
    vmem = pl.BlockSpec(memory_space=pltpu.VMEM)
    term = pltpu.VMEM((channels // 2, width_in), BF16)

    def in_hbm(array):
        return pltpu.with_memory_space_constraint(array, pltpu.HBM)

    return pl.pallas_call(
        functools.partial(term_kernel, piece, orders),
        out_shape=(term, term),
        in_specs=[pl.BlockSpec(memory_space=pltpu.SMEM), hbm, hbm, hbm, hbm],
        out_specs=(vmem, vmem),
        scratch_shapes=[
            pltpu.VMEM((rows, width_in), BF16),
            pltpu.VMEM((width_in, channels), BF16),
            pltpu.VMEM((1, channels), F32),
            pltpu.VMEM((rows, channels), BF16),
            pltpu.SemaphoreType.DMA((1 + 3 * (channels // piece),)),
        ],
        cost_estimate=pl.CostEstimate(
            flops=4 * rows * channels * width_in,
            bytes_accessed=2 * (rows * channels + channels * width_in * 2 + rows * width_in),
            transcendentals=channels,
        ),
        compiler_params=pltpu.CompilerParams(vmem_limit_bytes=16 * 2**20),
        name=name,
    )(parity.reshape(1), in_hbm(block_input), in_hbm(conv_weight), in_hbm(gain), in_hbm(out_cotangent))


def pick(array, index, axis=0):
    return lax.dynamic_index_in_dim(array, index, axis, keepdims=False)


def shift_pairs(size, shift):
    return [(i, (i + shift) % size) for i in range(size)]


def flip_pairs(size, bit):
    return [(i, i ^ bit) for i in range(size)]


def local_fn(block_input, conv_weight, bn_gain, out_cotangent, master_weight, velocity):
    nodes = lax.axis_size(NODE)
    lanes = lax.axis_size(LOCAL)
    width_in = block_input.shape[1]
    width_out = conv_weight.shape[1]
    run = width_out // nodes
    part = run // lanes
    depth = nodes // 4
    half = depth // 2
    node = lax.axis_index(NODE)
    lane = lax.axis_index(LOCAL)
    core = node % 2
    side = (node // 2) % 2
    deep = node // 4

    gain = bn_gain.reshape(1, width_out)
    piece = run
    if run % TILE:
        piece = width_out // 2

        def split(array):
            rows = array.shape[0]
            return array.reshape(rows, nodes // 2, 2, run).swapaxes(1, 2).reshape(rows, width_out)

        conv_weight, out_cotangent, gain = split(conv_weight), split(out_cotangent), split(gain)
    shapes = ((lanes, half, 2, part, width_in), (2, half, lanes, part, width_in))
    if part % PACK:
        whole = [(0, 0, width_out // 4)]
        orders = (whole, whole)
    else:
        orders = ([], [])
        for z in range(half):
            for y in range(2):
                for l in range(lanes):
                    source = (z * 2 + y) * run + l * part
                    orders[0].append((source, ((l * half + z) * 2 + y) * part, part))
                    orders[1].append((source, ((y * half + z) * lanes + l) * part, part))
    inputs = (block_input, conv_weight, gain, out_cotangent)
    far = terms(piece, orders, 1 - core, *inputs, name="far_terms")

    def laid(array, chunk):
        if part % PACK == 0:
            return array.reshape(shapes[chunk])
        array = array.reshape(half, 2, lanes, part, width_in)
        return array.transpose((2, 0, 1, 3, 4) if chunk == 0 else (1, 0, 2, 3, 4))

    got = [laid(lax.ppermute(array, NODE, flip_pairs(nodes, 1)), c) for c, array in enumerate(far)]
    own = terms(piece, orders, core, *inputs, name="own_terms")
    own = [laid(array, c) for c, array in enumerate(own)]

    def chip(chunk, index):
        return pick(own[chunk], index).astype(F32) + pick(got[chunk], index).astype(F32)

    def over_lane(send, keep):
        arrived = [
            lax.ppermute(send((lane + s) % lanes).astype(BF16), LOCAL, shift_pairs(lanes, s))
            for s in range(1, lanes)
        ]
        total = keep(lane)
        for piece_ in arrived:
            total = total + piece_.astype(F32)
        return total

    def over_side(send, keep):
        arrived = lax.ppermute(send(1 - side).astype(BF16), NODE, flip_pairs(nodes, 2))
        return keep(side) + arrived.astype(F32)

    take = functools.partial(chip, 0)
    first = over_lane(take, take)
    take = functools.partial(chip, 1)
    second = over_side(take, take)
    take = functools.partial(pick, first, axis=1)
    first = over_side(take, take)
    take = functools.partial(pick, second, axis=1)
    second = over_lane(take, take)

    plane = jnp.concatenate([first, second], axis=0)
    total = pick(plane, deep)
    for s in range(1, depth):
        piece_ = pick(plane, (deep + s) % depth).astype(BF16)
        total = total + lax.ppermute(piece_, NODE, shift_pairs(nodes, 4 * s)).astype(F32)

    total = total.astype(BF16)
    pieces = [total] + [
        lax.ppermute(total, LOCAL, shift_pairs(lanes, -s)) for s in range(1, lanes)
    ]
    gradient = jnp.concatenate(
        [
            functools.reduce(
                lambda other, s: jnp.where((lane + s) % lanes == l, pieces[s], other),
                range(1, lanes),
                pieces[0],
            )
            for l in range(lanes)
        ],
        axis=0,
    ).astype(F32)
    new_velocity = MOMENTUM * velocity + gradient + DECAY * master_weight
    new_weight = master_weight - RATE * new_velocity
    return (new_velocity, new_weight)


def solution(mesh):
    in_specs = (
        P((NODE, LOCAL), None),
        P(),
        P(),
        P((NODE, LOCAL), None),
        P(NODE, None),
        P(NODE, None),
    )
    out_specs = (P(NODE, None), P(NODE, None))
    return jax.shard_map(local_fn, mesh=mesh, in_specs=in_specs, out_specs=out_specs, check_vma=False)
```

```python
import functools

import jax
import jax.numpy as jnp
from jax import lax
from jax.experimental import pallas as pl
from jax.experimental.pallas import tpu as pltpu
from jax.sharding import PartitionSpec as P

EPS = 1e-05
MOMENTUM = 0.9
RATE = 0.1
DECAY = 5e-05

TILE = 128
NODE = "node"
LOCAL = "local"
F32 = jnp.float32
BF16 = jnp.bfloat16


def term_kernel(
    piece, column, blocks, parity_ref, half_ref, x_hbm, w_hbm, gain_hbm, u_hbm, *refs
):
    *out_refs, x_ref, w_ref, gain_ref, u_ref, conv_ref, grad_ref, sem = refs
    parity, half = parity_ref[0], half_ref[0]
    rows = x_hbm.shape[0]
    channels = w_ref.shape[1]
    block = channels // blocks

    copies = [pltpu.make_async_copy(x_hbm, x_ref, sem.at[0])]
    for k in range(channels // piece):
        source = pl.ds(pl.multiple_of(column(k, parity, half) * piece, piece), piece)
        target = pl.ds(k * piece, piece)
        for a, b in ((w_hbm, w_ref), (u_hbm, u_ref), (gain_hbm, gain_ref)):
            copies.append(pltpu.make_async_copy(a.at[:, source], b.at[:, target], sem.at[len(copies)]))
    for copy in copies:
        copy.start()
    for copy in copies:
        copy.wait()

    def columns(b):
        return slice(b * block, (b + 1) * block)

    def convolve(b):
        conv_ref[b] = jnp.dot(x_ref[...], w_ref[:, columns(b)], preferred_element_type=F32)

    def differentiate(b):
        conv = conv_ref[b]
        center = jnp.sum(conv, axis=0, keepdims=True) * (1.0 / rows)
        spread = conv - center
        upstream = u_ref[:, columns(b)].astype(F32)
        inverse = lax.rsqrt(jnp.sum(spread * spread, axis=0, keepdims=True) * (1.0 / rows) + EPS)
        shift_grad = jnp.sum(upstream, axis=0, keepdims=True)
        gain_grad = jnp.sum(upstream * spread, axis=0, keepdims=True) * inverse
        scale = gain_ref[:, columns(b)] * inverse
        step = scale * (1.0 / rows)
        grad = scale * upstream - (step * shift_grad + spread * (step * inverse * gain_grad))
        grad_ref[b] = grad.astype(BF16)

    def contract(b):
        term = lax.dot_general(
            grad_ref[b], x_ref[...], (((0,), (0,)), ((), ())), preferred_element_type=F32
        ).astype(BF16)
        share = channels // len(out_refs)
        count = min(block, share)
        for row in range(0, block, count):
            to, at = divmod(b * block + row, share)
            out_refs[to][at : at + count] = term[row : row + count]

    for i in range(blocks + 2):
        if 0 <= i - 2:
            contract(i - 2)
        if i < blocks:
            convolve(i)
        if 0 <= i - 1 < blocks:
            differentiate(i - 1)


def terms(name, outs, channels, blocks, piece, column, weight, parity, half, block_input, conv_weight, gain, out_cotangent):
    rows, width_in = block_input.shape
    block = channels // blocks
    hbm = pl.BlockSpec(memory_space=pltpu.HBM)
    smem = pl.BlockSpec(memory_space=pltpu.SMEM)

    def in_hbm(array):
        return pltpu.with_memory_space_constraint(array, pltpu.HBM)

    return pl.pallas_call(
        functools.partial(term_kernel, piece, column, blocks),
        out_shape=(pltpu.VMEM((channels // outs, width_in), BF16),) * outs,
        in_specs=[smem, smem, hbm, hbm, hbm, hbm],
        out_specs=(pl.BlockSpec(memory_space=pltpu.VMEM),) * outs,
        scratch_shapes=[
            pltpu.VMEM((rows, width_in), BF16),
            pltpu.VMEM((width_in, channels), BF16),
            pltpu.VMEM((1, channels), F32),
            pltpu.VMEM((rows, channels), BF16),
            pltpu.VMEM((blocks, rows, block), F32),
            pltpu.VMEM((blocks, rows, block), BF16),
            pltpu.SemaphoreType.DMA((1 + 3 * (channels // piece),)),
        ],
        cost_estimate=pl.CostEstimate(
            flops=max(1, int(weight * 4 * rows * channels * width_in)),
            bytes_accessed=max(1, int(weight * 2 * (rows * channels + channels * width_in * 2 + rows * width_in))),
            transcendentals=max(1, int(weight * channels)),
        ),
        compiler_params=pltpu.CompilerParams(vmem_limit_bytes=16 * 2**20),
        name=name,
    )(
        parity.reshape(1),
        half.reshape(1),
        in_hbm(block_input),
        in_hbm(conv_weight),
        in_hbm(gain),
        in_hbm(out_cotangent),
    )


def pick(array, *index):
    start = [jnp.asarray(i).astype(jnp.uint32) for i in index]
    rest = array.shape[len(index) :]
    start += [jnp.uint32(0)] * len(rest)
    return lax.dynamic_slice(array, start, (1,) * len(index) + rest).reshape(rest)


def send(array, pairs):
    return lax.ppermute(array.astype(BF16), (NODE, LOCAL), pairs)


def wide(*arrays):
    return functools.reduce(lambda a, b: a + b, [a.astype(F32) for a in arrays])


def local_fn(block_input, conv_weight, bn_gain, out_cotangent, master_weight, velocity):
    nodes = lax.axis_size(NODE)
    lanes = lax.axis_size(LOCAL)
    run = conv_weight.shape[1] // nodes
    inputs = (block_input, conv_weight, bn_gain.reshape(1, -1), out_cotangent)
    if (nodes, lanes) == (16, 2) and run % TILE == 0:
        gradient, (master_weight, velocity) = sum_halves(run, *inputs, (master_weight, velocity))
    else:
        gradient = sum_lanes(run, *inputs)
    new_velocity = MOMENTUM * velocity + gradient + DECAY * master_weight
    new_weight = master_weight - RATE * new_velocity
    return (new_velocity, new_weight)


def sum_halves(run, block_input, conv_weight, gain, out_cotangent, state):
    width_in = block_input.shape[1]
    inputs = (block_input, conv_weight, gain, out_cotangent)
    node = lax.axis_index(NODE)
    core, side, low, high = node & 1, (node >> 1) & 1, (node >> 2) & 1, node >> 3
    is_one = core == 1
    first = jnp.where(is_one, low, side)
    second = jnp.where(is_one, side, low)

    def column(k, parity, half):
        half, k = (half, k) if k < 4 else (1 - half, k - 4)
        zero = (((k % 2) * 2 + k // 2) * 2 + half) * 2
        one = (((k % 2) * 2 + half) * 2 + k // 2) * 2 + 1
        return jnp.where(parity == 1, one, zero)

    def flip(array, zero, one):
        return send(array, [(i, i ^ (one if i & 2 else zero)) for i in range(32)])

    def node_terms(name, count, parity, half, weight):
        halves = count // 4
        return terms(name, halves, count * run, halves, run, column, weight, parity, half, *inputs)

    far_sent, far_kept = node_terms("far_terms", 8, 1 - core, 1 - second, 1)
    got_sent = flip(far_sent, 2, 2)
    got = flip(far_kept, 2, 2).reshape(2, 2, run, width_in)
    (own_sent,) = node_terms("own_sent", 4, core, 1 - first, 1)
    sent, core, kept = lax.optimization_barrier((wide(own_sent, got_sent).astype(BF16), core, first))
    arrived = flip(sent, 4, 8).reshape(2, 2, run, width_in)
    own = node_terms("own_kept", 4, core, kept, 1)[0].reshape(2, 2, run, width_in)

    def half_of(index):
        return wide(pick(own, index), pick(got, index), pick(arrived, index))

    again = flip(half_of(1 - second), 8, 4)
    plane = wide(half_of(second), again)
    plane, *state = lax.optimization_barrier((plane, *state))
    both = wide(pick(plane, high), flip(pick(plane, 1 - high), 16, 16)).astype(BF16)
    return wide(both, flip(both, 1, 1)), state


def sum_lanes(run, block_input, conv_weight, gain, out_cotangent):
    nodes = lax.axis_size(NODE)
    lanes = lax.axis_size(LOCAL)
    devices = nodes * lanes
    width_in = block_input.shape[1]
    width_out = conv_weight.shape[1]
    node = lax.axis_index(NODE)
    lane = lax.axis_index(LOCAL)
    core, side, deep = node % 2, (node // 2) % 2, node // 4
    depth = nodes // 4

    def split(array):
        rows = array.shape[0]
        return array.reshape(rows, nodes // 2, 2, run).swapaxes(1, 2).reshape(rows, width_out)

    inputs = (block_input, split(conv_weight), split(gain), split(out_cotangent))

    def chip_terms(name, parity):
        half = width_out // 2
        return terms(name, 1, half, 2, half, lambda k, parity, half: parity, 1, parity, parity, *inputs)[0]

    def laid(array):
        return array.reshape(depth, 2, lanes, run // lanes, width_in).transpose(2, 1, 0, 3, 4)

    got = laid(send(chip_terms("far_terms", 1 - core), [(i, i ^ lanes) for i in range(devices)]))
    own = laid(chip_terms("own_terms", core))
    half = wide(pick(own, lane), pick(got, lane))
    for s in range(1, lanes):
        to = (lane + s) % lanes
        pairs = [(i, i - i % lanes + (i + s) % lanes) for i in range(devices)]
        half = wide(half, send(wide(pick(own, to), pick(got, to)), pairs))
    other = send(pick(half, 1 - side), [(i, i ^ (2 * lanes)) for i in range(devices)])
    plane = wide(pick(half, side), other)
    total = pick(plane, deep)
    for s in range(1, depth):
        pairs = [(i, (i + 4 * s * lanes) % devices) for i in range(devices)]
        total = wide(total, send(pick(plane, (deep + s) % depth), pairs))
    total = total.astype(BF16)
    pieces = [total] + [
        send(total, [(i, i - i % lanes + (i - s) % lanes) for i in range(devices)]) for s in range(1, lanes)
    ]
    return jnp.concatenate(
        [
            functools.reduce(
                lambda other, s: jnp.where((lane + s) % lanes == l, pieces[s], other),
                range(1, lanes),
                pieces[0],
            )
            for l in range(lanes)
        ],
        axis=0,
    ).astype(F32)


def solution(mesh):
    in_specs = (
        P((NODE, LOCAL), None),
        P(),
        P(),
        P((NODE, LOCAL), None),
        P(NODE, None),
        P(NODE, None),
    )
    out_specs = (P(NODE, None), P(NODE, None))
    return jax.shard_map(local_fn, mesh=mesh, in_specs=in_specs, out_specs=out_specs, check_vma=False)
```

```python
import functools

import jax
import jax.numpy as jnp
from jax import lax
from jax.experimental import pallas as pl
from jax.experimental.pallas import tpu as pltpu
from jax.sharding import PartitionSpec as P

EPS = 1e-05
MOMENTUM = 0.9
RATE = 0.1
DECAY = 5e-05

TILE = 128
STREAMS = 2
NODE = "node"
LOCAL = "local"
F32 = jnp.float32
BF16 = jnp.bfloat16


def term_kernel(
    piece, streams, column, blocks, parity_ref, half_ref, x_hbm, w_hbm, gain_hbm, u_hbm, *refs
):
    *out_refs, x_ref, w_ref, gain_ref, u_ref, conv_ref, grad_ref, sem = refs
    parity, half = parity_ref[0], half_ref[0]
    rows = x_hbm.shape[0]
    channels = w_ref.shape[1]
    block = channels // blocks

    copies = [pltpu.make_async_copy(x_hbm, x_ref, sem.at[0])]
    for k in range(channels // piece):
        source = pl.ds(pl.multiple_of(column(k, parity, half) * piece, piece), piece)
        target = pl.ds(k * piece, piece)
        for a, b in ((w_hbm, w_ref), (u_hbm, u_ref), (gain_hbm, gain_ref)):
            copies.append(pltpu.make_async_copy(a.at[:, source], b.at[:, target], sem.at[len(copies)]))
    for copy in copies:
        copy.start()
    for copy in copies:
        copy.wait()

    def columns(b):
        return slice(b * block, (b + 1) * block)

    def convolve(b):
        conv_ref[b] = jnp.dot(x_ref[...], w_ref[:, columns(b)], preferred_element_type=F32)

    def differentiate(b):
        conv = conv_ref[b]
        center = jnp.sum(conv, axis=0, keepdims=True) * (1.0 / rows)
        spread = conv - center
        upstream = u_ref[:, columns(b)].astype(F32)
        inverse = lax.rsqrt(jnp.sum(spread * spread, axis=0, keepdims=True) * (1.0 / rows) + EPS)
        shift_grad = jnp.sum(upstream, axis=0, keepdims=True)
        gain_grad = jnp.sum(upstream * spread, axis=0, keepdims=True) * inverse
        scale = gain_ref[:, columns(b)] * inverse
        step = scale * (1.0 / rows)
        grad = scale * upstream - (step * shift_grad + spread * (step * inverse * gain_grad))
        grad_ref[b] = grad.astype(BF16)

    def contract(b):
        term = lax.dot_general(
            grad_ref[b], x_ref[...], (((0,), (0,)), ((), ())), preferred_element_type=F32
        ).astype(BF16)
        if streams == 1:
            out_refs[0][b * block : (b + 1) * block] = term
            return
        part = piece // streams
        for k in range(block // piece):
            for t in range(streams):
                row = k * piece + t * part
                out_refs[b * streams + t][k * part : (k + 1) * part] = term[row : row + part]

    for i in range(blocks + 2):
        if 0 <= i - 2:
            contract(i - 2)
        if i < blocks:
            convolve(i)
        if 0 <= i - 1 < blocks:
            differentiate(i - 1)


def terms(name, outs, channels, blocks, piece, streams, column, weight, parity, half, block_input, conv_weight, gain, out_cotangent):
    rows, width_in = block_input.shape
    block = channels // blocks
    hbm = pl.BlockSpec(memory_space=pltpu.HBM)
    smem = pl.BlockSpec(memory_space=pltpu.SMEM)

    def in_hbm(array):
        return pltpu.with_memory_space_constraint(array, pltpu.HBM)

    return pl.pallas_call(
        functools.partial(term_kernel, piece, streams, column, blocks),
        out_shape=(pltpu.VMEM((channels // outs, width_in), BF16),) * outs,
        in_specs=[smem, smem, hbm, hbm, hbm, hbm],
        out_specs=(pl.BlockSpec(memory_space=pltpu.VMEM),) * outs,
        scratch_shapes=[
            pltpu.VMEM((rows, width_in), BF16),
            pltpu.VMEM((width_in, channels), BF16),
            pltpu.VMEM((1, channels), F32),
            pltpu.VMEM((rows, channels), BF16),
            pltpu.VMEM((blocks, rows, block), F32),
            pltpu.VMEM((blocks, rows, block), BF16),
            pltpu.SemaphoreType.DMA((1 + 3 * (channels // piece),)),
        ],
        cost_estimate=pl.CostEstimate(
            flops=max(1, int(weight * 4 * rows * channels * width_in)),
            bytes_accessed=max(1, int(weight * 2 * (rows * channels + channels * width_in * 2 + rows * width_in))),
            transcendentals=max(1, int(weight * channels)),
        ),
        compiler_params=pltpu.CompilerParams(vmem_limit_bytes=16 * 2**20),
        name=name,
    )(
        parity.reshape(1),
        half.reshape(1),
        in_hbm(block_input),
        in_hbm(conv_weight),
        in_hbm(gain),
        in_hbm(out_cotangent),
    )


def pick(array, *index):
    start = [jnp.asarray(i).astype(jnp.uint32) for i in index]
    rest = array.shape[len(index) :]
    start += [jnp.uint32(0)] * len(rest)
    return lax.dynamic_slice(array, start, (1,) * len(index) + rest).reshape(rest)


def send(array, pairs):
    return lax.ppermute(array.astype(BF16), (NODE, LOCAL), pairs)


def wide(*arrays):
    return functools.reduce(lambda a, b: a + b, [a.astype(F32) for a in arrays])


def local_fn(block_input, conv_weight, bn_gain, out_cotangent, master_weight, velocity):
    nodes = lax.axis_size(NODE)
    lanes = lax.axis_size(LOCAL)
    run = conv_weight.shape[1] // nodes
    inputs = (block_input, conv_weight, bn_gain.reshape(1, -1), out_cotangent)
    if (nodes, lanes) == (16, 2) and run % TILE == 0:
        gradient, (master_weight, velocity) = sum_halves(run, *inputs, (master_weight, velocity))
    else:
        gradient = sum_lanes(run, *inputs)
    new_velocity = MOMENTUM * velocity + gradient + DECAY * master_weight
    new_weight = master_weight - RATE * new_velocity
    return (new_velocity, new_weight)


def sum_halves(run, block_input, conv_weight, gain, out_cotangent, state):
    width_in = block_input.shape[1]
    inputs = (block_input, conv_weight, gain, out_cotangent)
    node = lax.axis_index(NODE)
    core, side, low, high = node & 1, (node >> 1) & 1, (node >> 2) & 1, node >> 3
    is_one = core == 1
    first = jnp.where(is_one, low, side)
    second = jnp.where(is_one, side, low)

    def column(k, parity, half):
        half, k = (half, k) if k < 4 else (1 - half, k - 4)
        zero = (((k % 2) * 2 + k // 2) * 2 + half) * 2
        one = (((k % 2) * 2 + half) * 2 + k // 2) * 2 + 1
        return jnp.where(parity == 1, one, zero)

    def flip(array, zero, one):
        return send(array, [(i, i ^ (one if i & 2 else zero)) for i in range(32)])

    def node_terms(name, count, parity, half, weight):
        halves = count // 4
        return terms(name, halves * STREAMS, count * run, halves, run, STREAMS, column, weight, parity, half, *inputs)

    part = run // STREAMS

    def laid(arrays):
        return [array.reshape(2, 2, part, width_in) for array in arrays]

    far = node_terms("far_terms", 8, 1 - core, 1 - second, 1)
    got_sent = [flip(array, 2, 2) for array in far[:STREAMS]]
    got = laid([flip(array, 2, 2) for array in far[STREAMS:]])
    own_sent = node_terms("own_sent", 4, core, 1 - first, 1)
    sent = [wide(*pair).astype(BF16) for pair in zip(own_sent, got_sent)]
    sent, core, kept = lax.optimization_barrier((sent, core, first))
    arrived = laid([flip(array, 4, 8) for array in sent])
    own = laid(node_terms("own_kept", 4, core, kept, 1))

    def half_of(t, index):
        return wide(pick(own[t], index), pick(got[t], index), pick(arrived[t], index))

    again = [flip(half_of(t, 1 - second), 8, 4) for t in range(STREAMS)]
    planes = [wide(half_of(t, second), again[t]) for t in range(STREAMS)]
    planes[0], *state = lax.optimization_barrier((planes[0], *state))
    both = [wide(pick(plane, high), flip(pick(plane, 1 - high), 16, 16)).astype(BF16) for plane in planes]
    return jnp.concatenate([wide(array, flip(array, 1, 1)) for array in both], axis=0), state


def sum_lanes(run, block_input, conv_weight, gain, out_cotangent):
    nodes = lax.axis_size(NODE)
    lanes = lax.axis_size(LOCAL)
    devices = nodes * lanes
    width_in = block_input.shape[1]
    width_out = conv_weight.shape[1]
    node = lax.axis_index(NODE)
    lane = lax.axis_index(LOCAL)
    core, side, deep = node % 2, (node // 2) % 2, node // 4
    depth = nodes // 4

    def split(array):
        rows = array.shape[0]
        return array.reshape(rows, nodes // 2, 2, run).swapaxes(1, 2).reshape(rows, width_out)

    inputs = (block_input, split(conv_weight), split(gain), split(out_cotangent))

    def chip_terms(name, parity):
        half = width_out // 2
        return terms(name, 1, half, 2, half, 1, lambda k, parity, half: parity, 1, parity, parity, *inputs)[0]

    def laid(array):
        return array.reshape(depth, 2, lanes, run // lanes, width_in).transpose(2, 1, 0, 3, 4)

    got = laid(send(chip_terms("far_terms", 1 - core), [(i, i ^ lanes) for i in range(devices)]))
    own = laid(chip_terms("own_terms", core))
    half = wide(pick(own, lane), pick(got, lane))
    for s in range(1, lanes):
        to = (lane + s) % lanes
        pairs = [(i, i - i % lanes + (i + s) % lanes) for i in range(devices)]
        half = wide(half, send(wide(pick(own, to), pick(got, to)), pairs))
    other = send(pick(half, 1 - side), [(i, i ^ (2 * lanes)) for i in range(devices)])
    plane = wide(pick(half, side), other)
    total = pick(plane, deep)
    for s in range(1, depth):
        pairs = [(i, (i + 4 * s * lanes) % devices) for i in range(devices)]
        total = wide(total, send(pick(plane, (deep + s) % depth), pairs))
    total = total.astype(BF16)
    pieces = [total] + [
        send(total, [(i, i - i % lanes + (i - s) % lanes) for i in range(devices)]) for s in range(1, lanes)
    ]
    return jnp.concatenate(
        [
            functools.reduce(
                lambda other, s: jnp.where((lane + s) % lanes == l, pieces[s], other),
                range(1, lanes),
                pieces[0],
            )
            for l in range(lanes)
        ],
        axis=0,
    ).astype(F32)


def solution(mesh):
    in_specs = (
        P((NODE, LOCAL), None),
        P(),
        P(),
        P((NODE, LOCAL), None),
        P(NODE, None),
        P(NODE, None),
    )
    out_specs = (P(NODE, None), P(NODE, None))
    return jax.shard_map(local_fn, mesh=mesh, in_specs=in_specs, out_specs=out_specs, check_vma=False)
```

```python
import functools

import jax
import jax.numpy as jnp
from jax import lax
from jax.experimental import pallas as pl
from jax.experimental.pallas import tpu as pltpu
from jax.sharding import PartitionSpec as P

EPS = 1e-05
MOMENTUM = 0.9
RATE = 0.1
DECAY = 5e-05

TILE = 128
STREAMS = (4, 4)
NODE = "node"
LOCAL = "local"
F32 = jnp.float32
BF16 = jnp.bfloat16


def term_rows(piece, parts, blocks, out_refs, x_ref, w_ref, gain_ref, u_ref, conv_ref, grad_ref):
    rows, channels = u_ref.shape
    block = channels // blocks

    def columns(b):
        return slice(b * block, (b + 1) * block)

    def convolve(b):
        conv_ref[b] = jnp.dot(x_ref[...], w_ref[:, columns(b)], preferred_element_type=F32)

    def differentiate(b):
        conv = conv_ref[b]
        center = jnp.sum(conv, axis=0, keepdims=True) * (1.0 / rows)
        spread = conv - center
        upstream = u_ref[:, columns(b)].astype(F32)
        inverse = lax.rsqrt(jnp.sum(spread * spread, axis=0, keepdims=True) * (1.0 / rows) + EPS)
        shift_grad = jnp.sum(upstream, axis=0, keepdims=True)
        gain_grad = jnp.sum(upstream * spread, axis=0, keepdims=True) * inverse
        scale = gain_ref[:, columns(b)] * inverse
        step = scale * (1.0 / rows)
        grad = scale * upstream - (step * shift_grad + spread * (step * inverse * gain_grad))
        grad_ref[b] = grad.astype(BF16)

    def contract(b):
        term = lax.dot_general(
            grad_ref[b], x_ref[...], (((0,), (0,)), ((), ())), preferred_element_type=F32
        ).astype(BF16)
        if parts is None:
            out_refs[0][b * block : (b + 1) * block] = term
            return
        for k in range(block // piece):
            row = k * piece
            for t, part in enumerate(parts):
                out_refs[b * len(parts) + t][k * part : (k + 1) * part] = term[row : row + part]
                row += part

    for i in range(blocks + 2):
        if 0 <= i - 2:
            contract(i - 2)
        if i < blocks:
            convolve(i)
        if 0 <= i - 1 < blocks:
            differentiate(i - 1)


def reading_kernel(piece, column, next_column, parts, blocks, outs, parity_ref, half_ref, next_ref, *refs):
    hbm, out_refs, refs = refs[:4], refs[4 : 4 + outs], refs[4 + outs :]
    held = None
    if next_column is not None:
        x_ref, *held = refs[:4]
        *own, conv_ref, grad_ref, sem = refs[4:]
    else:
        x_ref, *own, conv_ref, grad_ref, sem = refs
    copies = [pltpu.make_async_copy(hbm[0], x_ref, sem.at[0])]
    used = 1

    def reads(to, column, *where):
        nonlocal used
        made = []
        for k in range(to[0].shape[1] // piece):
            source = pl.ds(pl.multiple_of(column(k, *where) * piece, piece), piece)
            for a, b in zip(hbm[1:], to):
                copy = pltpu.make_async_copy(a.at[:, source], b.at[:, pl.ds(k * piece, piece)], sem.at[used])
                made.append(copy)
                used += 1
        return made

    copies += reads(own, column, parity_ref[0], half_ref[0])
    later = [] if held is None else reads(held, next_column, 1 - parity_ref[0], next_ref[0])
    for copy in copies + later:
        copy.start()
    for copy in copies:
        copy.wait()
    term_rows(piece, parts, blocks, out_refs, x_ref, *own, conv_ref, grad_ref)
    for copy in later:
        copy.wait()


def holding_kernel(piece, parts, blocks, outs, *refs):
    term_rows(piece, parts, blocks, refs[4 : 4 + outs], *refs[:4], *refs[4 + outs :])


def term_call(name, inputs, channels, blocks, piece, parts, column=None, where=(), next_column=None, next_channels=0):
    rows, width_in = inputs[0].shape
    block = channels // blocks
    sizes = [channels] if parts is None else [part * (block // piece) for part in parts] * blocks
    hbm = pl.BlockSpec(memory_space=pltpu.HBM)
    vmem = pl.BlockSpec(memory_space=pltpu.VMEM)
    smem = pl.BlockSpec(memory_space=pltpu.SMEM)
    x = pltpu.VMEM((rows, width_in), BF16)
    outs = [pltpu.VMEM((size, width_in), BF16) for size in sizes]

    def read(count):
        return [pltpu.VMEM((width_in, count), BF16), pltpu.VMEM((1, count), F32), pltpu.VMEM((rows, count), BF16)]

    scratch = [pltpu.VMEM((blocks, rows, block), F32), pltpu.VMEM((blocks, rows, block), BF16)]
    if column is None:
        kernel = functools.partial(holding_kernel, piece, parts, blocks, len(outs))
        in_specs = [vmem] * 4
    else:
        kernel = functools.partial(reading_kernel, piece, column, next_column, parts, blocks, len(outs))
        in_specs = [smem] * 3 + [hbm] * 4
        inputs = [i.reshape(1) for i in where] + [pltpu.with_memory_space_constraint(a, pltpu.HBM) for a in inputs]
        scratch = read(channels) + scratch + [pltpu.SemaphoreType.DMA((1 + 3 * ((channels + next_channels) // piece),))]
        if next_column is None:
            scratch = [x] + scratch
        else:
            outs += [x] + read(next_channels)
    return pl.pallas_call(
        kernel,
        out_shape=tuple(outs),
        in_specs=in_specs,
        out_specs=(vmem,) * len(outs),
        scratch_shapes=scratch,
        cost_estimate=pl.CostEstimate(
            flops=4 * rows * channels * width_in,
            bytes_accessed=2 * (rows * channels + channels * width_in * 2 + rows * width_in),
            transcendentals=channels,
        ),
        compiler_params=pltpu.CompilerParams(vmem_limit_bytes=16 * 2**20),
        name=name,
    )(*inputs)


def pick(array, *index):
    start = [jnp.asarray(i).astype(jnp.uint32) for i in index]
    rest = array.shape[len(index) :]
    start += [jnp.uint32(0)] * len(rest)
    return lax.dynamic_slice(array, start, (1,) * len(index) + rest).reshape(rest)


def send(array, pairs):
    return lax.ppermute(array.astype(BF16), (NODE, LOCAL), pairs)


def wide(*arrays):
    return functools.reduce(lambda a, b: a + b, [a.astype(F32) for a in arrays])


def local_fn(block_input, conv_weight, bn_gain, out_cotangent, master_weight, velocity):
    nodes = lax.axis_size(NODE)
    lanes = lax.axis_size(LOCAL)
    run = conv_weight.shape[1] // nodes
    inputs = (block_input, conv_weight, bn_gain.reshape(1, -1), out_cotangent)
    if (nodes, lanes) == (16, 2) and run % TILE == 0:
        gradient, (master_weight, velocity) = sum_halves(run, *inputs, (master_weight, velocity))
    else:
        gradient = sum_lanes(run, *inputs)
    new_velocity = MOMENTUM * velocity + gradient + DECAY * master_weight
    new_weight = master_weight - RATE * new_velocity
    return (new_velocity, new_weight)


def sum_halves(run, block_input, conv_weight, gain, out_cotangent, state):
    width_in = block_input.shape[1]
    inputs = (block_input, conv_weight, gain, out_cotangent)
    node = lax.axis_index(NODE)
    core, side, low, high = node & 1, (node >> 1) & 1, (node >> 2) & 1, node >> 3
    is_one = core == 0
    first = jnp.where(is_one, low, side)
    second = jnp.where(is_one, side, low)

    def column(k, parity, half):
        half, k = (half, k) if k < 4 else (1 - half, k - 4)
        zero = (((k % 2) * 2 + k // 2) * 2 + half) * 2 + 1
        one = (((k % 2) * 2 + half) * 2 + k // 2) * 2
        return jnp.where(parity == 0, one, zero)

    def flip(array, zero, one):
        return send(array, [(i, i ^ (zero if i & 2 else one)) for i in range(32)])

    parts = [run * share // sum(STREAMS) for share in STREAMS]
    count = len(parts)

    def laid(arrays):
        return [array.reshape(2, 2, part, width_in) for array, part in zip(arrays, parts)]

    far = term_call(
        "far_terms", inputs, 8 * run, 2, run, parts, column, (1 - core, 1 - second, 1 - first), column, 4 * run
    )
    far, held = far[: 2 * count], far[2 * count :]
    got_sent = [flip(array, 2, 2) for array in far[:count]]
    got = laid([flip(array, 2, 2) for array in far[count:]])
    own_sent = term_call("own_sent", held, 4 * run, 1, run, parts)
    sent = [wide(*pair).astype(BF16) for pair in zip(own_sent, got_sent)]
    sent, core, kept = lax.optimization_barrier((sent, core, first))
    arrived = laid([flip(array, 4, 8) for array in sent])
    own = laid(term_call("own_kept", inputs, 4 * run, 1, run, parts, column, (core, kept, kept)))

    def half_of(t, index):
        return wide(pick(own[t], index), pick(got[t], index), pick(arrived[t], index))

    again = [flip(half_of(t, 1 - second), 8, 4) for t in range(count)]
    planes = [wide(half_of(t, second), again[t]) for t in range(count)]
    planes[0], *state = lax.optimization_barrier((planes[0], *state))
    both = [wide(pick(plane, high), flip(pick(plane, 1 - high), 16, 16)).astype(BF16) for plane in planes]
    return jnp.concatenate([wide(array, flip(array, 1, 1)) for array in both], axis=0), state


def sum_lanes(run, block_input, conv_weight, gain, out_cotangent):
    nodes = lax.axis_size(NODE)
    lanes = lax.axis_size(LOCAL)
    devices = nodes * lanes
    width_in = block_input.shape[1]
    width_out = conv_weight.shape[1]
    node = lax.axis_index(NODE)
    lane = lax.axis_index(LOCAL)
    core, side, deep = node % 2, (node // 2) % 2, node // 4
    depth = nodes // 4

    def split(array):
        rows = array.shape[0]
        return array.reshape(rows, nodes // 2, 2, run).swapaxes(1, 2).reshape(rows, width_out)

    inputs = (block_input, split(conv_weight), split(gain), split(out_cotangent))

    def chip_terms(name, parity):
        half = width_out // 2
        return term_call(name, inputs, half, 2, half, None, lambda k, parity, half: parity, (parity,) * 3)[0]

    def laid(array):
        return array.reshape(depth, 2, lanes, run // lanes, width_in).transpose(2, 1, 0, 3, 4)

    got = laid(send(chip_terms("far_terms", 1 - core), [(i, i ^ lanes) for i in range(devices)]))
    own = laid(chip_terms("own_terms", core))
    half = wide(pick(own, lane), pick(got, lane))
    for s in range(1, lanes):
        to = (lane + s) % lanes
        pairs = [(i, i - i % lanes + (i + s) % lanes) for i in range(devices)]
        half = wide(half, send(wide(pick(own, to), pick(got, to)), pairs))
    other = send(pick(half, 1 - side), [(i, i ^ (2 * lanes)) for i in range(devices)])
    plane = wide(pick(half, side), other)
    total = pick(plane, deep)
    for s in range(1, depth):
        pairs = [(i, (i + 4 * s * lanes) % devices) for i in range(devices)]
        total = wide(total, send(pick(plane, (deep + s) % depth), pairs))
    total = total.astype(BF16)
    pieces = [total] + [
        send(total, [(i, i - i % lanes + (i - s) % lanes) for i in range(devices)]) for s in range(1, lanes)
    ]
    return jnp.concatenate(
        [
            functools.reduce(
                lambda other, s: jnp.where((lane + s) % lanes == l, pieces[s], other),
                range(1, lanes),
                pieces[0],
            )
            for l in range(lanes)
        ],
        axis=0,
    ).astype(F32)


def solution(mesh):
    in_specs = (
        P((NODE, LOCAL), None),
        P(),
        P(),
        P((NODE, LOCAL), None),
        P(NODE, None),
        P(NODE, None),
    )
    out_specs = (P(NODE, None), P(NODE, None))
    return jax.shard_map(local_fn, mesh=mesh, in_specs=in_specs, out_specs=out_specs, check_vma=False)
```

```python
import functools

import jax
import jax.numpy as jnp
from jax import lax
from jax.experimental import pallas as pl
from jax.experimental.pallas import tpu as pltpu
from jax.sharding import PartitionSpec as P

EPS = 1e-05
MOMENTUM = 0.9
RATE = 0.1
DECAY = 5e-05

TILE = 128
STREAMS = (4, 4)
NODE = "node"
LOCAL = "local"
F32 = jnp.float32
BF16 = jnp.bfloat16


def term_rows(piece, parts, blocks, groups, out_refs, w_ref, gain_ref, conv_ref, grad_ref):
    rows, channels = groups[0][1].shape
    block = channels // blocks
    count = len(groups)

    def columns(b):
        return slice(b * block, (b + 1) * block)

    def convolve(i):
        b, g = divmod(i, count)
        conv_ref[i] = jnp.dot(groups[g][0][...], w_ref[:, columns(b)], preferred_element_type=F32)

    def differentiate(i):
        b, g = divmod(i, count)
        conv = conv_ref[i]
        center = jnp.sum(conv, axis=0, keepdims=True) * (1.0 / rows)
        spread = conv - center
        upstream = groups[g][1][:, columns(b)].astype(F32)
        inverse = lax.rsqrt(jnp.sum(spread * spread, axis=0, keepdims=True) * (1.0 / rows) + EPS)
        shift_grad = jnp.sum(upstream, axis=0, keepdims=True)
        gain_grad = jnp.sum(upstream * spread, axis=0, keepdims=True) * inverse
        scale = gain_ref[:, columns(b)] * inverse
        step = scale * (1.0 / rows)
        grad = scale * upstream - (step * shift_grad + spread * (step * inverse * gain_grad))
        grad_ref[i] = grad.astype(BF16)

    def contract(b):
        term = sum(
            lax.dot_general(
                grad_ref[b * count + g], groups[g][0][...], (((0,), (0,)), ((), ())), preferred_element_type=F32
            )
            for g in range(count)
        ).astype(BF16)
        if parts is None:
            out_refs[0][b * block : (b + 1) * block] = term
            return
        for k in range(block // piece):
            row = k * piece
            for t, part in enumerate(parts):
                out_refs[b * len(parts) + t][k * part : (k + 1) * part] = term[row : row + part]
                row += part

    for i in range(blocks * count + 2):
        if i >= 2 and (i - 1) % count == 0:
            contract((i - 1) // count - 1)
        if i < blocks * count:
            convolve(i)
        if 0 <= i - 1 < blocks * count:
            differentiate(i - 1)


def reading_kernel(piece, column, parts, blocks, outs, ahead, borrows, parity_ref, half_ref, next_ref, *refs):
    hbm, refs = refs[:4], refs[4:]
    width = hbm[0].shape[1]
    borrowed, refs = refs[:borrows], refs[borrows:]
    out_refs, refs = refs[:outs], refs[outs:]
    if ahead is not None:
        loan_ref, *held = refs[:4]
        refs = refs[4:]
        x_ref, lent_ref = loan_ref.at[:, pl.ds(0, width)], loan_ref.at[:, pl.ds(width, held[2].shape[1])]
    else:
        x_ref, *refs = refs
    w_ref, gain_ref, u_ref, *loans, conv_ref, grad_ref, sem = refs
    used = 0

    def read(a, b):
        nonlocal used
        used += 1
        return pltpu.make_async_copy(a, b, sem.at[used - 1])

    def reads(sources, targets, column, first, *where):
        made = []
        for k in range(targets[0].shape[1] // piece):
            at = pl.ds(pl.multiple_of(column(first + k, *where) * piece, piece), piece)
            made += [read(a.at[:, at], b.at[:, pl.ds(k * piece, piece)]) for a, b in zip(sources, targets)]
        return made

    here = parity_ref[0], half_ref[0]
    copies = [read(hbm[0], x_ref)] + reads(hbm[1:], (w_ref, gain_ref, u_ref), column, 0, *here)
    later = []
    groups = [(x_ref, u_ref)]
    if ahead is not None:
        later = reads(hbm[1:], held, ahead, 0, 1 - parity_ref[0], next_ref[0])
        later += reads(hbm[3:], [lent_ref], column, u_ref.shape[1] // piece, *here)
    for a, b in zip(borrowed, loans):
        copies.append(read(a, b))
        groups.append((b.at[:, pl.ds(0, width)], b.at[:, pl.ds(width, u_ref.shape[1])]))
    for copy in copies + later:
        copy.start()
    for copy in copies:
        copy.wait()
    term_rows(piece, parts, blocks, groups, out_refs, w_ref, gain_ref, conv_ref, grad_ref)
    for copy in later:
        copy.wait()


def holding_kernel(piece, parts, blocks, outs, loan_ref, w_ref, gain_ref, u_ref, *refs):
    x_ref = loan_ref.at[:, pl.ds(0, w_ref.shape[0])]
    term_rows(piece, parts, blocks, [(x_ref, u_ref)], refs[:outs], w_ref, gain_ref, *refs[outs:])


def term_call(name, inputs, channels, blocks, piece, parts, column=None, where=(), ahead=None, far=()):
    rows, width_in = inputs[0].shape[0], inputs[1].shape[0]
    block = channels // blocks
    groups = 2 if far else 1
    sizes = [channels] if parts is None else [part * (block // piece) for part in parts] * blocks
    hbm = pl.BlockSpec(memory_space=pltpu.HBM)
    vmem = pl.BlockSpec(memory_space=pltpu.VMEM)
    smem = pl.BlockSpec(memory_space=pltpu.SMEM)
    x = pltpu.VMEM((rows, width_in), BF16)
    loan = pltpu.VMEM((rows, width_in + channels), BF16)
    read = [pltpu.VMEM((width_in, channels), BF16), pltpu.VMEM((1, channels), F32), pltpu.VMEM((rows, channels), BF16)]
    outs = [pltpu.VMEM((size, width_in), BF16) for size in sizes]
    scratch = [pltpu.VMEM((blocks * groups, rows, block), F32), pltpu.VMEM((blocks * groups, rows, block), BF16)]
    if column is None:
        kernel = functools.partial(holding_kernel, piece, parts, blocks, len(outs))
        in_specs = [vmem] * 4
    else:
        kernel = functools.partial(reading_kernel, piece, column, parts, blocks, len(outs), ahead, len(far))
        in_specs = [smem] * 3 + [hbm] * 4 + [pl.BlockSpec(memory_space=pl.ANY)] * len(far)
        inputs = [pltpu.with_memory_space_constraint(a, pltpu.HBM) for a in inputs]
        inputs = [*(i.reshape(1) for i in where), *inputs, *far]
        pieces = channels // piece
        if ahead is None:
            scratch = [x, *read] + [loan] * len(far) + scratch + [pltpu.SemaphoreType.DMA((2 + 3 * pieces,))]
        else:
            outs += [loan, *read]
            scratch = read + scratch + [pltpu.SemaphoreType.DMA((1 + 7 * pieces,))]
    return pl.pallas_call(
        kernel,
        out_shape=tuple(outs),
        in_specs=in_specs,
        out_specs=(vmem,) * len(outs),
        scratch_shapes=scratch,
        cost_estimate=pl.CostEstimate(
            flops=4 * groups * rows * channels * width_in,
            bytes_accessed=2 * (groups * rows * (channels + width_in) + channels * width_in * 2),
            transcendentals=groups * channels,
        ),
        compiler_params=pltpu.CompilerParams(vmem_limit_bytes=16 * 2**20),
        name=name,
    )(*inputs)


def pick(array, *index):
    start = [jnp.asarray(i).astype(jnp.uint32) for i in index]
    rest = array.shape[len(index) :]
    start += [jnp.uint32(0)] * len(rest)
    return lax.dynamic_slice(array, start, (1,) * len(index) + rest).reshape(rest)


def send(array, pairs):
    return lax.ppermute(array.astype(BF16), (NODE, LOCAL), pairs)


def wide(*arrays):
    return functools.reduce(lambda a, b: a + b, [a.astype(F32) for a in arrays])


def local_fn(block_input, conv_weight, bn_gain, out_cotangent, master_weight, velocity):
    nodes = lax.axis_size(NODE)
    lanes = lax.axis_size(LOCAL)
    run = conv_weight.shape[1] // nodes
    inputs = (block_input, conv_weight, bn_gain.reshape(1, -1), out_cotangent)
    if (nodes, lanes) == (16, 2) and run % TILE == 0:
        gradient, (master_weight, velocity) = sum_halves(run, *inputs, (master_weight, velocity))
    else:
        gradient = sum_lanes(run, *inputs)
    new_velocity = MOMENTUM * velocity + gradient + DECAY * master_weight
    new_weight = master_weight - RATE * new_velocity
    return (new_velocity, new_weight)


def sum_halves(run, block_input, conv_weight, gain, out_cotangent, state):
    width_in = block_input.shape[1]
    inputs = (block_input, conv_weight, gain, out_cotangent)
    node = lax.axis_index(NODE)
    core, side, low, high = node & 1, (node >> 1) & 1, (node >> 2) & 1, node >> 3
    is_one = core == 0
    first = jnp.where(is_one, low, side)
    second = jnp.where(is_one, side, low)

    def column(k, parity, half):
        half, k = (half, k) if k < 4 else (1 - half, k - 4)
        zero = (((k % 2) * 2 + k // 2) * 2 + half) * 2 + 1
        one = (((k % 2) * 2 + half) * 2 + k // 2) * 2
        return jnp.where(parity == 0, one, zero)

    def flip(array, zero, one):
        return send(array, [(i, i ^ (zero if i & 2 else one)) for i in range(32)])

    parts = [run * share // sum(STREAMS) for share in STREAMS]
    count = len(parts)

    def laid(arrays):
        return [array.reshape(2, 2, part, width_in) for array, part in zip(arrays, parts)]

    *far_sent, loan, w, g, u = term_call(
        "far_sent", inputs, 4 * run, 1, run, parts, column, (1 - core, 1 - second, 1 - first), column
    )
    got_sent = jnp.split(flip(jnp.concatenate(far_sent, axis=0), 2, 2), len(parts), axis=0)
    far = (flip(loan, 2, 2),)
    own_sent = term_call("own_sent", (loan, w, g, u), 4 * run, 1, run, parts)
    sent = [wide(*pair).astype(BF16) for pair in zip(own_sent, got_sent)]
    sent, core, kept = lax.optimization_barrier((sent, core, first))
    arrived = laid([flip(array, 4, 8) for array in sent])
    own = laid(term_call("kept", inputs, 4 * run, 1, run, parts, column, (core, kept, kept), None, far))

    def half_of(t, index):
        return wide(pick(own[t], index), pick(arrived[t], index))

    again = [flip(half_of(t, 1 - second), 8, 4) for t in range(count)]
    planes = [wide(half_of(t, second), again[t]) for t in range(count)]
    planes[0], *state = lax.optimization_barrier((planes[0], *state))
    both = [wide(pick(plane, high), flip(pick(plane, 1 - high), 16, 16)).astype(BF16) for plane in planes]
    return jnp.concatenate([wide(array, flip(array, 1, 1)) for array in both], axis=0), state


def sum_lanes(run, block_input, conv_weight, gain, out_cotangent):
    nodes = lax.axis_size(NODE)
    lanes = lax.axis_size(LOCAL)
    devices = nodes * lanes
    width_in = block_input.shape[1]
    width_out = conv_weight.shape[1]
    node = lax.axis_index(NODE)
    lane = lax.axis_index(LOCAL)
    core, side, deep = node % 2, (node // 2) % 2, node // 4
    depth = nodes // 4

    def split(array):
        rows = array.shape[0]
        return array.reshape(rows, nodes // 2, 2, run).swapaxes(1, 2).reshape(rows, width_out)

    inputs = (block_input, split(conv_weight), split(gain), split(out_cotangent))

    def chip_terms(name, parity):
        half = width_out // 2
        return term_call(name, inputs, half, 2, half, None, lambda k, parity, half: parity, (parity,) * 3)[0]

    def laid(array):
        return array.reshape(depth, 2, lanes, run // lanes, width_in).transpose(2, 1, 0, 3, 4)

    got = laid(send(chip_terms("far_terms", 1 - core), [(i, i ^ lanes) for i in range(devices)]))
    own = laid(chip_terms("own_terms", core))
    half = wide(pick(own, lane), pick(got, lane))
    for s in range(1, lanes):
        to = (lane + s) % lanes
        pairs = [(i, i - i % lanes + (i + s) % lanes) for i in range(devices)]
        half = wide(half, send(wide(pick(own, to), pick(got, to)), pairs))
    other = send(pick(half, 1 - side), [(i, i ^ (2 * lanes)) for i in range(devices)])
    plane = wide(pick(half, side), other)
    total = pick(plane, deep)
    for s in range(1, depth):
        pairs = [(i, (i + 4 * s * lanes) % devices) for i in range(devices)]
        total = wide(total, send(pick(plane, (deep + s) % depth), pairs))
    total = total.astype(BF16)
    pieces = [total] + [
        send(total, [(i, i - i % lanes + (i - s) % lanes) for i in range(devices)]) for s in range(1, lanes)
    ]
    return jnp.concatenate(
        [
            functools.reduce(
                lambda other, s: jnp.where((lane + s) % lanes == l, pieces[s], other),
                range(1, lanes),
                pieces[0],
            )
            for l in range(lanes)
        ],
        axis=0,
    ).astype(F32)


def solution(mesh):
    in_specs = (
        P((NODE, LOCAL), None),
        P(),
        P(),
        P((NODE, LOCAL), None),
        P(NODE, None),
        P(NODE, None),
    )
    out_specs = (P(NODE, None), P(NODE, None))
    return jax.shard_map(local_fn, mesh=mesh, in_specs=in_specs, out_specs=out_specs, check_vma=False)
```

```python
import functools

import jax
import jax.numpy as jnp
from jax import lax
from jax.experimental import pallas as pl
from jax.experimental.pallas import tpu as pltpu
from jax.sharding import PartitionSpec as P

EPS = 1e-05
MOMENTUM = 0.9
RATE = 0.1
DECAY = 5e-05

TILE = 128
STREAMS = (4, 4)
NODE = "node"
LOCAL = "local"
F32 = jnp.float32
BF16 = jnp.bfloat16


def term_rows(piece, parts, blocks, groups, out_refs, w_ref, gain_ref, conv_ref, grad_ref):
    rows, channels = groups[0][1].shape
    block = channels // blocks
    count = len(groups)

    def columns(b):
        return slice(b * block, (b + 1) * block)

    def convolve(i):
        b, g = divmod(i, count)
        conv_ref[i] = jnp.dot(groups[g][0][...], w_ref[:, columns(b)], preferred_element_type=F32)

    def differentiate(i):
        b, g = divmod(i, count)
        conv = conv_ref[i]
        center = jnp.sum(conv, axis=0, keepdims=True) * (1.0 / rows)
        spread = conv - center
        upstream = groups[g][1][:, columns(b)].astype(F32)
        inverse = lax.rsqrt(jnp.sum(spread * spread, axis=0, keepdims=True) * (1.0 / rows) + EPS)
        shift_grad = jnp.sum(upstream, axis=0, keepdims=True)
        gain_grad = jnp.sum(upstream * spread, axis=0, keepdims=True) * inverse
        scale = gain_ref[:, columns(b)] * inverse
        step = scale * (1.0 / rows)
        grad = scale * upstream - (step * shift_grad + spread * (step * inverse * gain_grad))
        grad_ref[i] = grad.astype(BF16)

    def contract(b):
        term = sum(
            lax.dot_general(
                grad_ref[b * count + g], groups[g][0][...], (((0,), (0,)), ((), ())), preferred_element_type=F32
            )
            for g in range(count)
        ).astype(BF16)
        if parts is None:
            out_refs[0][b * block : (b + 1) * block] = term
            return
        for k in range(block // piece):
            row = k * piece
            for t, part in enumerate(parts):
                out_refs[b * len(parts) + t][k * part : (k + 1) * part] = term[row : row + part]
                row += part

    for i in range(blocks * count + 2):
        if i >= 2 and (i - 1) % count == 0:
            contract((i - 1) // count - 1)
        if i < blocks * count:
            convolve(i)
        if 0 <= i - 1 < blocks * count:
            differentiate(i - 1)


def reading_kernel(piece, column, parts, blocks, outs, ahead, borrows, parity_ref, half_ref, next_ref, *refs):
    hbm, refs = refs[:4], refs[4:]
    width = hbm[0].shape[1]
    borrowed, refs = refs[:borrows], refs[borrows:]
    out_refs, refs = refs[:outs], refs[outs:]
    if ahead is not None:
        loan_ref, *held = refs[:4]
        refs = refs[4:]
        x_ref, lent_ref = loan_ref.at[:, pl.ds(0, width)], loan_ref.at[:, pl.ds(width, held[2].shape[1])]
    else:
        x_ref, *refs = refs
    w_ref, gain_ref, u_ref, *loans, conv_ref, grad_ref, sem = refs
    copies, waits = [], []

    def read(target, *pairs):
        done = sem.at[len(waits)]
        copies.extend(pltpu.make_async_copy(a, b, done) for a, b in pairs)
        waits.append(pltpu.make_async_copy(target, target, done))

    def reads(sources, targets, column, first, *where):
        at = [
            pl.ds(pl.multiple_of(column(first + k, *where) * piece, piece), piece)
            for k in range(targets[0].shape[1] // piece)
        ]
        for a, b in zip(sources, targets):
            read(b, *((a.at[:, there], b.at[:, pl.ds(k * piece, piece)]) for k, there in enumerate(at)))

    here = parity_ref[0], half_ref[0]
    read(x_ref, (hbm[0], x_ref))
    reads(hbm[1:], (w_ref, gain_ref, u_ref), column, 0, *here)
    groups = [(x_ref, u_ref)]
    for a, b in zip(borrowed, loans):
        read(b, (a, b))
        groups.append((b.at[:, pl.ds(0, width)], b.at[:, pl.ds(width, u_ref.shape[1])]))
    needed = len(waits)
    if ahead is not None:
        reads(hbm[1:], held, ahead, 0, 1 - parity_ref[0], next_ref[0])
        reads(hbm[3:], [lent_ref], column, u_ref.shape[1] // piece, *here)
    for copy in copies:
        copy.start()
    for wait in waits[:needed]:
        wait.wait()
    term_rows(piece, parts, blocks, groups, out_refs, w_ref, gain_ref, conv_ref, grad_ref)
    for wait in waits[needed:]:
        wait.wait()


def holding_kernel(piece, parts, blocks, outs, loan_ref, w_ref, gain_ref, u_ref, *refs):
    x_ref = loan_ref.at[:, pl.ds(0, w_ref.shape[0])]
    term_rows(piece, parts, blocks, [(x_ref, u_ref)], refs[:outs], w_ref, gain_ref, *refs[outs:])


def term_call(name, inputs, channels, blocks, piece, parts, column=None, where=(), ahead=None, far=()):
    rows, width_in = inputs[0].shape[0], inputs[1].shape[0]
    block = channels // blocks
    groups = 2 if far else 1
    sizes = [channels] if parts is None else [part * (block // piece) for part in parts] * blocks
    hbm = pl.BlockSpec(memory_space=pltpu.HBM)
    vmem = pl.BlockSpec(memory_space=pltpu.VMEM)
    smem = pl.BlockSpec(memory_space=pltpu.SMEM)
    x = pltpu.VMEM((rows, width_in), BF16)
    loan = pltpu.VMEM((rows, width_in + channels), BF16)
    read = [pltpu.VMEM((width_in, channels), BF16), pltpu.VMEM((1, channels), F32), pltpu.VMEM((rows, channels), BF16)]
    outs = [pltpu.VMEM((size, width_in), BF16) for size in sizes]
    scratch = [pltpu.VMEM((blocks * groups, rows, block), F32), pltpu.VMEM((blocks * groups, rows, block), BF16)]
    if column is None:
        kernel = functools.partial(holding_kernel, piece, parts, blocks, len(outs))
        in_specs = [vmem] * 4
    else:
        kernel = functools.partial(reading_kernel, piece, column, parts, blocks, len(outs), ahead, len(far))
        in_specs = [smem] * 3 + [hbm] * 4 + [pl.BlockSpec(memory_space=pl.ANY)] * len(far)
        inputs = [pltpu.with_memory_space_constraint(a, pltpu.HBM) for a in inputs]
        inputs = [*(i.reshape(1) for i in where), *inputs, *far]
        if ahead is None:
            scratch = [x, *read] + [loan] * len(far) + scratch + [pltpu.SemaphoreType.DMA((4 + len(far),))]
        else:
            outs += [loan, *read]
            scratch = read + scratch + [pltpu.SemaphoreType.DMA((8,))]
    return pl.pallas_call(
        kernel,
        out_shape=tuple(outs),
        in_specs=in_specs,
        out_specs=(vmem,) * len(outs),
        scratch_shapes=scratch,
        cost_estimate=pl.CostEstimate(
            flops=4 * groups * rows * channels * width_in,
            bytes_accessed=2 * (groups * rows * (channels + width_in) + channels * width_in * 2),
            transcendentals=groups * channels,
        ),
        compiler_params=pltpu.CompilerParams(vmem_limit_bytes=16 * 2**20),
        name=name,
    )(*inputs)


def update_kernel(part, rows, grad_ref, rest_ref, velocity_ref, weight_ref, *refs):
    new_velocity_hbm, new_weight_hbm, new_velocity_ref, new_weight_ref, sem = refs[-5:]
    at = pl.ds(rows * part, part)
    weight = weight_ref[at, :]
    gradient = grad_ref[...].astype(F32) + rest_ref[...].astype(F32)
    new_velocity = MOMENTUM * velocity_ref[at, :] + gradient + DECAY * weight
    new_velocity_ref[...] = new_velocity
    first = pltpu.make_async_copy(new_velocity_ref, new_velocity_hbm.at[at, :], sem.at[0])
    first.start()
    new_weight_ref[...] = weight - RATE * new_velocity
    second = pltpu.make_async_copy(new_weight_ref, new_weight_hbm.at[at, :], sem.at[1])
    second.start()
    first.wait()
    second.wait()


def update_call(rows, grad, rest, velocity, weight, previous):
    part, width_in = grad.shape
    vmem = pl.BlockSpec(memory_space=pltpu.VMEM)
    hbm = pl.BlockSpec(memory_space=pltpu.HBM)
    return pl.pallas_call(
        functools.partial(update_kernel, part, rows),
        out_shape=(jax.ShapeDtypeStruct(velocity.shape, F32),) * 2,
        in_specs=[vmem] * 4 + [hbm] * len(previous),
        out_specs=(hbm, hbm),
        scratch_shapes=[pltpu.VMEM((part, width_in), F32)] * 2 + [pltpu.SemaphoreType.DMA((2,))],
        input_output_aliases={4 + i: i for i in range(len(previous))},
        compiler_params=pltpu.CompilerParams(vmem_limit_bytes=4 * 2**20),
        name="update",
    )(grad, rest, velocity, weight, *previous)


def pick(array, *index):
    start = [jnp.asarray(i).astype(jnp.uint32) for i in index]
    rest = array.shape[len(index) :]
    start += [jnp.uint32(0)] * len(rest)
    return lax.dynamic_slice(array, start, (1,) * len(index) + rest).reshape(rest)


def send(array, pairs):
    return lax.ppermute(array.astype(BF16), (NODE, LOCAL), pairs)


def wide(*arrays):
    return functools.reduce(lambda a, b: a + b, [a.astype(F32) for a in arrays])


def local_fn(block_input, conv_weight, bn_gain, out_cotangent, master_weight, velocity):
    nodes = lax.axis_size(NODE)
    lanes = lax.axis_size(LOCAL)
    run = conv_weight.shape[1] // nodes
    inputs = (block_input, conv_weight, bn_gain.reshape(1, -1), out_cotangent)
    if (nodes, lanes) == (16, 2) and run % TILE == 0:
        return step_halves(run, *inputs, master_weight, velocity)
    gradient = sum_lanes(run, *inputs)
    new_velocity = MOMENTUM * velocity + gradient + DECAY * master_weight
    new_weight = master_weight - RATE * new_velocity
    return (new_velocity, new_weight)


def step_halves(run, block_input, conv_weight, gain, out_cotangent, master_weight, velocity):
    width_in = block_input.shape[1]
    inputs = (block_input, conv_weight, gain, out_cotangent)
    node = lax.axis_index(NODE)
    core, side, low, high = node & 1, (node >> 1) & 1, (node >> 2) & 1, node >> 3
    is_zero = core == 0
    first = jnp.where(is_zero, low, side)
    second = jnp.where(is_zero, side, low)

    def column(k, parity, half):
        half, k = (half, k) if k < 4 else (1 - half, k - 4)
        zero = (((k % 2) * 2 + k // 2) * 2 + half) * 2 + 1
        one = (((k % 2) * 2 + half) * 2 + k // 2) * 2
        return jnp.where(parity == 0, one, zero)

    def flip(array, zero, one):
        return send(array, [(i, i ^ (zero if i & 2 else one)) for i in range(32)])

    parts = [run * share // sum(STREAMS) for share in STREAMS]
    count = len(parts)

    def laid(arrays):
        return [array.reshape(2, 2, part, width_in) for array, part in zip(arrays, parts)]

    *far_sent, loan, w, g, u = term_call(
        "far_sent", inputs, 4 * run, 1, run, parts, column, (1 - core, 1 - second, 1 - first), column
    )
    got_sent = jnp.split(flip(jnp.concatenate(far_sent, axis=0), 2, 2), len(parts), axis=0)
    far = (flip(loan, 2, 2),)
    own_sent = term_call("own_sent", (loan, w, g, u), 4 * run, 1, run, parts)
    sent = [wide(*pair).astype(BF16) for pair in zip(own_sent, got_sent)]
    sent, core, kept = lax.optimization_barrier((sent, core, first))
    arrived = laid([flip(array, 4, 8) for array in sent])
    own = laid(term_call("kept", inputs, 4 * run, 1, run, parts, column, (core, kept, kept), None, far))

    def half_of(t, index):
        return wide(pick(own[t], index), pick(arrived[t], index))

    again = [flip(half_of(t, 1 - second), 8, 4) for t in range(count)]
    planes = [wide(half_of(t, second), again[t]) for t in range(count)]
    planes[0], velocity, master_weight = lax.optimization_barrier((planes[0], velocity, master_weight))
    both = [wide(pick(plane, high), flip(pick(plane, 1 - high), 16, 16)).astype(BF16) for plane in planes]
    out = ()
    for t, array in enumerate(both):
        out = update_call(t, array, flip(array, 1, 1), velocity, master_weight, out)
    return out


def sum_lanes(run, block_input, conv_weight, gain, out_cotangent):
    nodes = lax.axis_size(NODE)
    lanes = lax.axis_size(LOCAL)
    devices = nodes * lanes
    width_in = block_input.shape[1]
    width_out = conv_weight.shape[1]
    node = lax.axis_index(NODE)
    lane = lax.axis_index(LOCAL)
    core, side, deep = node % 2, (node // 2) % 2, node // 4
    depth = nodes // 4

    def split(array):
        rows = array.shape[0]
        return array.reshape(rows, nodes // 2, 2, run).swapaxes(1, 2).reshape(rows, width_out)

    inputs = (block_input, split(conv_weight), split(gain), split(out_cotangent))

    def chip_terms(name, parity):
        half = width_out // 2
        return term_call(name, inputs, half, 2, half, None, lambda k, parity, half: parity, (parity,) * 3)[0]

    def laid(array):
        return array.reshape(depth, 2, lanes, run // lanes, width_in).transpose(2, 1, 0, 3, 4)

    got = laid(send(chip_terms("far_terms", 1 - core), [(i, i ^ lanes) for i in range(devices)]))
    own = laid(chip_terms("own_terms", core))
    half = wide(pick(own, lane), pick(got, lane))
    for s in range(1, lanes):
        to = (lane + s) % lanes
        pairs = [(i, i - i % lanes + (i + s) % lanes) for i in range(devices)]
        half = wide(half, send(wide(pick(own, to), pick(got, to)), pairs))
    other = send(pick(half, 1 - side), [(i, i ^ (2 * lanes)) for i in range(devices)])
    plane = wide(pick(half, side), other)
    total = pick(plane, deep)
    for s in range(1, depth):
        pairs = [(i, (i + 4 * s * lanes) % devices) for i in range(devices)]
        total = wide(total, send(pick(plane, (deep + s) % depth), pairs))
    total = total.astype(BF16)
    pieces = [total] + [
        send(total, [(i, i - i % lanes + (i - s) % lanes) for i in range(devices)]) for s in range(1, lanes)
    ]
    return jnp.concatenate(
        [
            functools.reduce(
                lambda other, s: jnp.where((lane + s) % lanes == l, pieces[s], other),
                range(1, lanes),
                pieces[0],
            )
            for l in range(lanes)
        ],
        axis=0,
    ).astype(F32)


def solution(mesh):
    in_specs = (
        P((NODE, LOCAL), None),
        P(),
        P(),
        P((NODE, LOCAL), None),
        P(NODE, None),
        P(NODE, None),
    )
    out_specs = (P(NODE, None), P(NODE, None))
    return jax.shard_map(local_fn, mesh=mesh, in_specs=in_specs, out_specs=out_specs, check_vma=False)
```

```python
import functools

import jax
import jax.numpy as jnp
from jax import lax
from jax.experimental import pallas as pl
from jax.experimental.pallas import tpu as pltpu
from jax.sharding import PartitionSpec as P

EPS = 1e-05
MOMENTUM = 0.9
RATE = 0.1
DECAY = 5e-05

TILE = 128
STREAMS = (4, 4)
NODE = "node"
LOCAL = "local"
F32 = jnp.float32
BF16 = jnp.bfloat16


def term_rows(piece, parts, blocks, groups, out_refs, w_ref, gain_ref, conv_ref, grad_ref):
    rows, channels = groups[0][1].shape
    block = channels // blocks
    count = len(groups)

    def columns(b):
        return slice(b * block, (b + 1) * block)

    def convolve(i):
        b, g = divmod(i, count)
        conv_ref[i] = jnp.dot(groups[g][0][...], w_ref[:, columns(b)], preferred_element_type=F32)

    def differentiate(i):
        b, g = divmod(i, count)
        conv = conv_ref[i]
        center = jnp.sum(conv, axis=0, keepdims=True) * (1.0 / rows)
        spread = conv - center
        upstream = groups[g][1][:, columns(b)].astype(F32)
        inverse = lax.rsqrt(jnp.sum(spread * spread, axis=0, keepdims=True) * (1.0 / rows) + EPS)
        shift_grad = jnp.sum(upstream, axis=0, keepdims=True)
        gain_grad = jnp.sum(upstream * spread, axis=0, keepdims=True) * inverse
        scale = gain_ref[:, columns(b)] * inverse
        step = scale * (1.0 / rows)
        grad = scale * upstream - (step * shift_grad + spread * (step * inverse * gain_grad))
        grad_ref[i] = grad.astype(BF16)

    def contract(b):
        term = sum(
            lax.dot_general(
                grad_ref[b * count + g], groups[g][0][...], (((0,), (0,)), ((), ())), preferred_element_type=F32
            )
            for g in range(count)
        ).astype(BF16)
        if parts is None:
            out_refs[0][b * block : (b + 1) * block] = term
            return
        for k in range(block // piece):
            row = k * piece
            for t, part in enumerate(parts):
                out_refs[b * len(parts) + t][k * part : (k + 1) * part] = term[row : row + part]
                row += part

    for i in range(blocks * count + 2):
        if i >= 2 and (i - 1) % count == 0:
            contract((i - 1) // count - 1)
        if i < blocks * count:
            convolve(i)
        if 0 <= i - 1 < blocks * count:
            differentiate(i - 1)


def reading_kernel(piece, column, parts, blocks, outs, ahead, borrows, parity_ref, half_ref, next_ref, *refs):
    hbm, refs = refs[:4], refs[4:]
    width = hbm[0].shape[1]
    borrowed, refs = refs[:borrows], refs[borrows:]
    out_refs, refs = refs[:outs], refs[outs:]
    if ahead is not None:
        loan_ref, *held = refs[:4]
        refs = refs[4:]
        x_ref, lent_ref = loan_ref.at[:, pl.ds(0, width)], loan_ref.at[:, pl.ds(width, held[2].shape[1])]
    else:
        x_ref, *refs = refs
    w_ref, gain_ref, u_ref, *loans, conv_ref, grad_ref, sem = refs
    copies, waits = [], []

    def read(target, *pairs):
        done = sem.at[len(waits)]
        copies.extend(pltpu.make_async_copy(a, b, done) for a, b in pairs)
        waits.append(pltpu.make_async_copy(target, target, done))

    def reads(sources, targets, column, first, *where):
        at = [
            pl.ds(pl.multiple_of(column(first + k, *where) * piece, piece), piece)
            for k in range(targets[0].shape[1] // piece)
        ]
        for a, b in zip(sources, targets):
            read(b, *((a.at[:, there], b.at[:, pl.ds(k * piece, piece)]) for k, there in enumerate(at)))

    here = parity_ref[0], half_ref[0]
    read(x_ref, (hbm[0], x_ref))
    reads(hbm[1:], (w_ref, gain_ref, u_ref), column, 0, *here)
    groups = [(x_ref, u_ref)]
    for a, b in zip(borrowed, loans):
        read(b, (a, b))
        groups.append((b.at[:, pl.ds(0, width)], b.at[:, pl.ds(width, u_ref.shape[1])]))
    needed = len(waits)
    if ahead is not None:
        reads(hbm[1:], held, ahead, 0, 1 - parity_ref[0], next_ref[0])
        reads(hbm[3:], [lent_ref], column, u_ref.shape[1] // piece, *here)
    for copy in copies:
        copy.start()
    for wait in waits[:needed]:
        wait.wait()
    term_rows(piece, parts, blocks, groups, out_refs, w_ref, gain_ref, conv_ref, grad_ref)
    for wait in waits[needed:]:
        wait.wait()


def holding_kernel(piece, parts, blocks, outs, loan_ref, w_ref, gain_ref, u_ref, *refs):
    x_ref = loan_ref.at[:, pl.ds(0, w_ref.shape[0])]
    term_rows(piece, parts, blocks, [(x_ref, u_ref)], refs[:outs], w_ref, gain_ref, *refs[outs:])


def term_call(name, inputs, channels, blocks, piece, parts, column=None, where=(), ahead=None, far=()):
    rows, width_in = inputs[0].shape[0], inputs[1].shape[0]
    block = channels // blocks
    groups = 2 if far else 1
    sizes = [channels] if parts is None else [part * (block // piece) for part in parts] * blocks
    hbm = pl.BlockSpec(memory_space=pltpu.HBM)
    vmem = pl.BlockSpec(memory_space=pltpu.VMEM)
    smem = pl.BlockSpec(memory_space=pltpu.SMEM)
    x = pltpu.VMEM((rows, width_in), BF16)
    loan = pltpu.VMEM((rows, width_in + channels), BF16)
    read = [pltpu.VMEM((width_in, channels), BF16), pltpu.VMEM((1, channels), F32), pltpu.VMEM((rows, channels), BF16)]
    outs = [pltpu.VMEM((size, width_in), BF16) for size in sizes]
    scratch = [pltpu.VMEM((blocks * groups, rows, block), F32), pltpu.VMEM((blocks * groups, rows, block), BF16)]
    if column is None:
        kernel = functools.partial(holding_kernel, piece, parts, blocks, len(outs))
        in_specs = [vmem] * 4
    else:
        kernel = functools.partial(reading_kernel, piece, column, parts, blocks, len(outs), ahead, len(far))
        in_specs = [smem] * 3 + [hbm] * 4 + [pl.BlockSpec(memory_space=pl.ANY)] * len(far)
        inputs = [pltpu.with_memory_space_constraint(a, pltpu.HBM) for a in inputs]
        inputs = [*(i.reshape(1) for i in where), *inputs, *far]
        if ahead is None:
            scratch = [x, *read] + [loan] * len(far) + scratch + [pltpu.SemaphoreType.DMA((4 + len(far),))]
        else:
            outs += [loan, *read]
            scratch = read + scratch + [pltpu.SemaphoreType.DMA((8,))]
    return pl.pallas_call(
        kernel,
        out_shape=tuple(outs),
        in_specs=in_specs,
        out_specs=(vmem,) * len(outs),
        scratch_shapes=scratch,
        cost_estimate=pl.CostEstimate(
            flops=4 * groups * rows * channels * width_in,
            bytes_accessed=2 * (groups * rows * (channels + width_in) + channels * width_in * 2),
            transcendentals=groups * channels,
        ),
        compiler_params=pltpu.CompilerParams(vmem_limit_bytes=16 * 2**20),
        name=name,
    )(*inputs)


def update_kernel(part, rows, grad_ref, rest_ref, velocity_ref, weight_ref, *refs):
    new_velocity_hbm, new_weight_hbm, new_velocity_ref, new_weight_ref, sem = refs[-5:]
    at = pl.ds(rows * part, part)
    weight = weight_ref[at, :]
    gradient = grad_ref[...].astype(F32) + rest_ref[...].astype(F32)
    new_velocity = MOMENTUM * velocity_ref[at, :] + gradient + DECAY * weight
    new_velocity_ref[...] = new_velocity
    first = pltpu.make_async_copy(new_velocity_ref, new_velocity_hbm.at[at, :], sem.at[0])
    first.start()
    new_weight_ref[...] = weight - RATE * new_velocity
    second = pltpu.make_async_copy(new_weight_ref, new_weight_hbm.at[at, :], sem.at[1])
    second.start()
    first.wait()
    second.wait()


def update_call(rows, grad, rest, velocity, weight, previous):
    part, width_in = grad.shape
    vmem = pl.BlockSpec(memory_space=pltpu.VMEM)
    hbm = pl.BlockSpec(memory_space=pltpu.HBM)
    return pl.pallas_call(
        functools.partial(update_kernel, part, rows),
        out_shape=(jax.ShapeDtypeStruct(velocity.shape, F32),) * 2,
        in_specs=[vmem] * 4 + [hbm] * len(previous),
        out_specs=(hbm, hbm),
        scratch_shapes=[pltpu.VMEM((part, width_in), F32)] * 2 + [pltpu.SemaphoreType.DMA((2,))],
        input_output_aliases={4 + i: i for i in range(len(previous))},
        compiler_params=pltpu.CompilerParams(vmem_limit_bytes=4 * 2**20),
        name="update",
    )(grad, rest, velocity, weight, *previous)


def pick(array, *index):
    start = [jnp.asarray(i).astype(jnp.uint32) for i in index]
    rest = array.shape[len(index) :]
    start += [jnp.uint32(0)] * len(rest)
    return lax.dynamic_slice(array, start, (1,) * len(index) + rest).reshape(rest)


def send(array, pairs):
    return lax.ppermute(array.astype(BF16), (NODE, LOCAL), pairs)


def wide(*arrays):
    return functools.reduce(lambda a, b: a + b, [a.astype(F32) for a in arrays])


def local_fn(block_input, conv_weight, bn_gain, out_cotangent, master_weight, velocity):
    nodes = lax.axis_size(NODE)
    lanes = lax.axis_size(LOCAL)
    run = conv_weight.shape[1] // nodes
    inputs = (block_input, conv_weight, bn_gain.reshape(1, -1), out_cotangent)
    if (nodes, lanes) == (16, 2) and run % TILE == 0:
        return step_halves(run, *inputs, master_weight, velocity)
    gradient = sum_lanes(run, *inputs)
    new_velocity = MOMENTUM * velocity + gradient + DECAY * master_weight
    new_weight = master_weight - RATE * new_velocity
    return (new_velocity, new_weight)


def step_halves(run, block_input, conv_weight, gain, out_cotangent, master_weight, velocity):
    width_in = block_input.shape[1]
    inputs = (block_input, conv_weight, gain, out_cotangent)
    node = lax.axis_index(NODE)
    core, side, low, high = node & 1, (node >> 1) & 1, (node >> 2) & 1, node >> 3
    is_zero = core == 0
    first = jnp.where(is_zero, low, side)
    second = jnp.where(is_zero, side, low)

    def column(k, parity, half):
        half, k = (half, k) if k < 4 else (1 - half, k - 4)
        one = (((k % 2) * 2 + k // 2) * 2 + half) * 2 + 1
        zero = (((k % 2) * 2 + half) * 2 + k // 2) * 2
        return jnp.where(parity == 1, one, zero)

    def flip(array, one, zero):
        return send(array, [(i, i ^ (one if i & 2 else zero)) for i in range(32)])

    parts = [run * share // sum(STREAMS) for share in STREAMS]
    count = len(parts)

    def laid(arrays):
        return [array.reshape(2, 2, part, width_in) for array, part in zip(arrays, parts)]

    *far_sent, loan, w, g, u = term_call(
        "far_sent", inputs, 4 * run, 1, run, parts, column, (1 - core, 1 - second, 1 - first), column
    )
    got_sent = jnp.split(flip(jnp.concatenate(far_sent, axis=0), 2, 2), len(parts), axis=0)
    far = (flip(loan, 2, 2),)
    own_sent = term_call("own_sent", (loan, w, g, u), 4 * run, 1, run, parts)
    sent = [wide(*pair).astype(BF16) for pair in zip(own_sent, got_sent)]
    sent, core, kept = lax.optimization_barrier((sent, core, first))
    arrived = laid([flip(array, 4, 8) for array in sent])
    own = laid(term_call("kept", inputs, 4 * run, 1, run, parts, column, (core, kept, kept), None, far))

    def half_of(t, index):
        return wide(pick(own[t], index), pick(arrived[t], index))

    again = [flip(half_of(t, 1 - second), 8, 4) for t in range(count)]

    def plane(t, index):
        return wide(pick(own[t], second, index), pick(arrived[t], second, index), pick(again[t], index))

    away = [plane(t, 1 - high).astype(BF16) for t in range(count)]
    away[0], velocity, master_weight = lax.optimization_barrier((away[0], velocity, master_weight))
    both = [wide(plane(t, high), flip(away[t], 16, 16)).astype(BF16) for t in range(count)]
    out = ()
    for t, array in enumerate(both):
        out = update_call(t, array, flip(array, 1, 1), velocity, master_weight, out)
    return out


def sum_lanes(run, block_input, conv_weight, gain, out_cotangent):
    nodes = lax.axis_size(NODE)
    lanes = lax.axis_size(LOCAL)
    devices = nodes * lanes
    width_in = block_input.shape[1]
    width_out = conv_weight.shape[1]
    node = lax.axis_index(NODE)
    lane = lax.axis_index(LOCAL)
    core, side, deep = node % 2, (node // 2) % 2, node // 4
    depth = nodes // 4

    def split(array):
        rows = array.shape[0]
        return array.reshape(rows, nodes // 2, 2, run).swapaxes(1, 2).reshape(rows, width_out)

    inputs = (block_input, split(conv_weight), split(gain), split(out_cotangent))

    def chip_terms(name, parity):
        half = width_out // 2
        return term_call(name, inputs, half, 2, half, None, lambda k, parity, half: parity, (parity,) * 3)[0]

    def laid(array):
        return array.reshape(depth, 2, lanes, run // lanes, width_in).transpose(2, 1, 0, 3, 4)

    got = laid(send(chip_terms("far_terms", 1 - core), [(i, i ^ lanes) for i in range(devices)]))
    own = laid(chip_terms("own_terms", core))
    half = wide(pick(own, lane), pick(got, lane))
    for s in range(1, lanes):
        to = (lane + s) % lanes
        pairs = [(i, i - i % lanes + (i + s) % lanes) for i in range(devices)]
        half = wide(half, send(wide(pick(own, to), pick(got, to)), pairs))
    other = send(pick(half, 1 - side), [(i, i ^ (2 * lanes)) for i in range(devices)])
    plane = wide(pick(half, side), other)
    total = pick(plane, deep)
    for s in range(1, depth):
        pairs = [(i, (i + 4 * s * lanes) % devices) for i in range(devices)]
        total = wide(total, send(pick(plane, (deep + s) % depth), pairs))
    total = total.astype(BF16)
    pieces = [total] + [
        send(total, [(i, i - i % lanes + (i - s) % lanes) for i in range(devices)]) for s in range(1, lanes)
    ]
    return jnp.concatenate(
        [
            functools.reduce(
                lambda other, s: jnp.where((lane + s) % lanes == l, pieces[s], other),
                range(1, lanes),
                pieces[0],
            )
            for l in range(lanes)
        ],
        axis=0,
    ).astype(F32)


def solution(mesh):
    in_specs = (
        P((NODE, LOCAL), None),
        P(),
        P(),
        P((NODE, LOCAL), None),
        P(NODE, None),
        P(NODE, None),
    )
    out_specs = (P(NODE, None), P(NODE, None))
    return jax.shard_map(local_fn, mesh=mesh, in_specs=in_specs, out_specs=out_specs, check_vma=False)
```
